32 devices in a mesh: chan: 8 (over y, x, core), cross: 4 (over z).
Axes of the slice: x: 2, y: 2, z: 4, core: 2. Of those that a mesh axis runs over, the one named last changes fastest.
Arguments:
- positions: float32 [2, 32, 64, 128], P(None, 'chan', 'cross'), may hold values from 0 to 1
- velocity: float32 [2, 32, 64, 128], P(None, 'chan', 'cross'), may hold values from -4 to 4
- density: float32 [32, 64, 128], P('chan', 'cross'), may hold values from 0.8 to 1.2
- counts: int32 [32, 64], P('chan', 'cross'), may hold values from 0 to 128, as said below
Outputs:
- new_fields: float32 [5, 32, 64, 128], P(None, 'chan', 'cross')
- lowest_density: float32 [], replicated
The draws below stay inside these ranges and needn't reach their ends.
Inputs may be any that keep to these rules, and one draw needn't show every extreme that they name: `counts`: in every channel column the bins from cross index 0 up to some height hold particles and those above are empty; the height is 56 or more; the bins at cross index 0 hold 128 particles.
All inputs are finite; a program needn't handle non-finite values.
Results may differ from the reference program's by a relative error of at most 0.0001.
Values sent between devices are 32-bit elements; how exact they have to be, the bound alone decides.
A program may use at most 64 MiB of HBM per device.

```python
import math
import jax
import jax.numpy as jnp
from jax import lax

S = 128
BY = 16
NBX = 32
NBY = 64


def draw_density(key, part):
    key_phase, key_jitter = jax.random.split(jax.random.fold_in(key, 11))
    along_axis = jnp.arange(NBX, dtype=jnp.float32) / NBX
    across = jnp.arange(NBY, dtype=jnp.float32) / NBY
    wave_phase = jax.random.uniform(key_phase, (), jnp.float32, 0.0, 2.0 * math.pi)
    amplitude = 0.08
    jitter = jax.random.uniform(key_jitter, (NBX, NBY, S), jnp.float32, -0.03, 0.03)
    wave_term = amplitude * jnp.sin(2.0 * math.pi * along_axis + wave_phase)
    return 1.0 + wave_term[:, None, None] + 0.04 * (1.0 - across)[None, :, None] + jitter


def draw_counts(key, part):
    key_height, key_fill = jax.random.split(jax.random.fold_in(key, 23))
    height = jax.random.randint(key_height, (NBX,), NBY - BY // 2, NBY + 1)
    occupancy = jax.random.randint(key_fill, (NBX, NBY), 64, S + 1)
    row_index = jnp.arange(NBY)
    counts = jnp.where(row_index[None, :] < height[:, None], occupancy, 0)
    return jnp.where(row_index[None, :] == 0, S, counts).astype(jnp.int32)


def steps_of(key, dims, shards, low, top_value):
    def one(position, parts):
        heights = jax.random.uniform(jax.random.fold_in(jax.random.fold_in(key, 6), position), (parts,), jnp.float32, low / len(shards), top_value / len(shards))
        return jnp.repeat(jnp.exp(heights), dims[position] // parts).reshape((-1,) + (1,) * (len(dims) - position - 1))

    factor_of = one(*shards[0])
    for cut in shards[1:]:
        factor_of = factor_of * one(*cut)
    return factor_of


def scatter_about(stream_key, shape, scale, limit, cuts=(), held_as=jnp.bfloat16):
    entries = scale * jax.random.normal(stream_key, shape, jnp.float32)
    if cuts:
        entries = entries * steps_of(stream_key, shape, cuts, -0.22, 0.18)
    return jnp.clip(entries, -limit, limit).astype(held_as)


def setup_inputs(seed: int = 0) -> dict:
    keys = jax.random.split(jax.random.key(seed), 5)
    positions = jnp.clip(1.0 * jax.random.uniform(keys[0], (2, NBX, NBY, S), jnp.float32) ** steps_of(keys[0], (2, NBX, NBY, S), ((1, 8), (2, 4)), -0.2, 0.2), 0.0, 1.0)
    velocity = scatter_about(keys[1], (2, NBX, NBY, S), 1.0, 4.0, ((1, 8), (2, 4)), jnp.float32)
    density = draw_density(jax.random.fold_in(keys[4], 71), 0)
    counts = draw_counts(jax.random.fold_in(keys[4], 71), 0)
    return dict(positions=positions, velocity=velocity, density=density, counts=counts)


FAR_SHIFT = 8.0
SOUND_SQ = 100.0
KERNEL_GRAD = 140.0 / math.pi
PARTICLE_MASS = 1.0 / 128.0
GRAVITY = 1.0
TIME_STEP = 0.025

def pack_fields(positions, velocity, density, occupied):
    return jnp.stack([(positions[0] + FAR_SHIFT) * occupied, (positions[1] + FAR_SHIFT) * occupied, velocity[0] * occupied, velocity[1] * occupied, density * occupied])

def column_rates(window):
    bin_rows = window.shape[2] - 2
    centre = window[:, 1, 1:bin_rows + 1]
    centre_pressure = SOUND_SQ * (centre[4] - 1.0)
    force_x = jnp.zeros_like(centre[0])
    force_y = jnp.zeros_like(centre[0])
    compress = jnp.zeros_like(centre[0])
    for offset_col in (-1, 0, 1):
        for offset_row in (-1, 0, 1):
            neighbour = window[:, 1 + offset_col, 1 + offset_row:1 + offset_row + bin_rows]
            delta_x = centre[0][:, :, None] - neighbour[0][:, None, :] - offset_col
            delta_y = centre[1][:, :, None] - neighbour[1][:, None, :] - offset_row
            radius = jnp.sqrt(delta_x * delta_x + delta_y * delta_y)
            weight = jnp.maximum(1.0 - radius, 0.0) ** 3
            pressure = (centre_pressure[:, :, None] + SOUND_SQ * (neighbour[4][:, None, :] - 1.0)) * weight
            force_x = force_x + lax.optimization_barrier(jnp.sum(pressure * delta_x, axis=2))
            force_y = force_y + lax.optimization_barrier(jnp.sum(pressure * delta_y, axis=2))
            closing = (centre[2][:, :, None] - neighbour[2][:, None, :]) * delta_x + (centre[3][:, :, None] - neighbour[3][:, None, :]) * delta_y
            compress = compress + lax.optimization_barrier(jnp.sum(weight * closing, axis=2))
    force_scale = KERNEL_GRAD * PARTICLE_MASS
    return jnp.stack([force_scale * force_x, force_scale * force_y - GRAVITY, -force_scale * compress])

def all_rates(fields):
    padded = jnp.concatenate([fields[:, -1:], fields, fields[:, :1]], axis=1)
    padded = jnp.pad(padded, ((0, 0), (0, 0), (1, 1), (0, 0)))
    columns = jnp.arange(fields.shape[1], dtype=jnp.int32)

    def one_column(column):
        return column_rates(lax.dynamic_slice_in_dim(padded, column, 3, 1))
    per_column = lax.map(one_column, columns)
    return jnp.transpose(per_column, (1, 0, 2, 3))

def reference(positions, velocity, density, counts):
    slot_index = jnp.arange(positions.shape[-1], dtype=jnp.int32)
    occupied = (slot_index[None, None, :] < counts[:, :, None]).astype(jnp.float32)
    fields = pack_fields(positions, velocity, density, occupied)
    first_rates = all_rates(fields)
    half_step = 0.5 * TIME_STEP
    predicted = jnp.stack([fields[0] + half_step * fields[2], fields[1] + half_step * fields[3], fields[2] + half_step * first_rates[0], fields[3] + half_step * first_rates[1], fields[4] + half_step * first_rates[2]]) * occupied
    second_rates = all_rates(predicted)
    final_ux = fields[2] + TIME_STEP * second_rates[0]
    final_uy = fields[3] + TIME_STEP * second_rates[1]
    final_x = fields[0] + half_step * (fields[2] + final_ux) - FAR_SHIFT
    final_y = fields[1] + half_step * (fields[3] + final_uy) - FAR_SHIFT
    final_density = fields[4] + TIME_STEP * second_rates[2]
    new_fields = jnp.stack([final_x, final_y, final_ux, final_uy, final_density]) * occupied
    lowest = jnp.min(jnp.where(occupied > 0.0, final_density, 1000000000.0))
    return (new_fields, lowest)
```

```python
import functools
import math

import jax
import jax.numpy as jnp
from jax import lax
from jax.experimental import pallas as pl
from jax.experimental.pallas import tpu as pltpu
from jax.sharding import PartitionSpec as P

FAR_SHIFT = 8.0
SOUND_SQ = 100.0
KERNEL_GRAD = 140.0 / math.pi
PARTICLE_MASS = 1.0 / 128.0
GRAVITY = 1.0
TIME_STEP = 0.025
FORCE_SCALE = KERNEL_GRAD * PARTICLE_MASS
EMPTY_DENSITY = 1000000000.0

FEATURES = 9
QROWS = 32


def exchange(x, sides):
    for axis, dim in sides:
        size, length = (lax.axis_size(axis), x.shape[dim])
        up = [(i, (i + 1) % size) for i in range(size)]
        down = [(j, i) for i, j in up]
        last = lax.slice_in_dim(x, length - 1, length, axis=dim)
        leading = lax.slice_in_dim(x, 0, 1, axis=dim)
        before = lax.ppermute(last, axis, up)
        after = lax.ppermute(leading, axis, down)
        x = jnp.concatenate([before, x, after], axis=dim)
    return x


def extend_rims(fields):
    extended = exchange(fields, (("chan", 1), ("cross", 2)))
    cross_place = lax.axis_index("cross")
    cross_count = lax.axis_size("cross")
    rim_row = jnp.arange(extended.shape[2], dtype=jnp.int32)
    lower_open = jnp.logical_or(rim_row != 0, cross_place > 0)
    upper_open = jnp.logical_or(rim_row != extended.shape[2] - 1, cross_place < cross_count - 1)
    wall_keep = jnp.logical_and(lower_open, upper_open).astype(jnp.float32)
    return extended * wall_keep[None, None, :, None]


def split3(value):
    high = value.astype(jnp.bfloat16).astype(jnp.float32)
    rest = value - high
    middle = rest.astype(jnp.bfloat16).astype(jnp.float32)
    return high, middle, rest - middle


def rates_kernel(final, *refs):
    if final:
        padded, base, out, low, px, py, staged, feats, sums = refs
    else:
        padded, out, px, py, staged, feats, sums = refs
    _, pcols, prows, slots = padded.shape
    cols, rows = pcols - 2, prows - 2
    mid_col, mid_row = (pcols - 1) / 2.0, (prows - 1) / 2.0

    row_shift = lax.broadcasted_iota(jnp.int32, (prows, slots), 0).astype(jnp.float32) - mid_row
    staged[...] = jnp.zeros_like(staged)
    for c in range(pcols):
        x = (padded[0, c] - (FAR_SHIFT + 0.5)) + (c - mid_col)
        y = (padded[1, c] - (FAR_SHIFT + 0.5)) + row_shift
        u, v = padded[2, c], padded[3, c]
        p = SOUND_SQ * (padded[4, c] - 1.0)
        px[c] = x
        py[c] = y
        staged[:, 0, :] = jnp.ones_like(x)
        for f, value in enumerate((x, y, p, p * x, p * y, u, v, u * x + v * y)):
            for k, part in enumerate(split3(value)):
                staged[:, 1 + 3 * f + k, :] = part
        for j in range(prows):
            feats[c, :, j * slots : (j + 1) * slots] = staged[j].astype(jnp.bfloat16)

    def one_bin(n, carry):
        i = n // rows
        j = n % rows
        xa = jnp.broadcast_to(px[i + 1, pl.ds(j + 1, 1), :], (slots, slots)).T
        ya = jnp.broadcast_to(py[i + 1, pl.ds(j + 1, 1), :], (slots, slots)).T
        total = None
        for di in range(3):
            highs, lows = [], []
            for dj in range(3):
                dx = xa - px[i + di, pl.ds(j + dj, 1), :]
                dy = ya - py[i + di, pl.ds(j + dj, 1), :]
                d2 = jnp.maximum(dx * dx + dy * dy, 1e-30)
                s = jnp.maximum(1.0 - d2 * lax.rsqrt(d2), 0.0)
                w = s * s * s
                high = w.astype(jnp.bfloat16)
                highs.append(high)
                lows.append((w - high.astype(jnp.float32)).astype(jnp.bfloat16))
            q = feats[i + di, :, pl.ds(pl.multiple_of(j * slots, slots), 3 * slots)]
            part = lax.dot_general(
                jnp.concatenate(highs + lows, axis=1),
                jnp.concatenate([q, q], axis=1),
                (((1,), (1,)), ((), ())),
                preferred_element_type=jnp.float32,
            )
            total = part if total is None else total + part
        sums[n] = total.T
        return carry

    lax.fori_loop(0, cols * rows, one_bin, 0)

    lowest = None
    for i in range(cols):
        def take(f):
            block = pl.ds(i * rows, rows)
            if f == 0:
                return sums[block, 0, :]
            first = 1 + 3 * (f - 1)
            return sums[block, first, :] + (sums[block, first + 1, :] + sums[block, first + 2, :])

        s1, sx, sy, sp, spx, spy, su, sv, sc = [take(f) for f in range(FEATURES)]
        own = pl.ds(1, rows)
        x, y = px[i + 1, own, :], py[i + 1, own, :]
        u, v = padded[2, i + 1, own, :], padded[3, i + 1, own, :]
        p = SOUND_SQ * (padded[4, i + 1, own, :] - 1.0)
        away_x, away_y = x * s1 - sx, y * s1 - sy
        force_x = FORCE_SCALE * (p * away_x + (x * sp - spx))
        force_y = FORCE_SCALE * (p * away_y + (y * sp - spy)) - GRAVITY
        compress = -FORCE_SCALE * ((u * away_x + v * away_y) - (x * su + y * sv) + sc)
        occupied = padded[0, i + 1, own, :] > 0.5 * FAR_SHIFT
        half_step = 0.5 * TIME_STEP
        if final:
            bx, by, bu, bv, br = [base[k, i] for k in range(5)]
            new_u = bu + TIME_STEP * force_x
            new_v = bv + TIME_STEP * force_y
            new_rho = br + TIME_STEP * compress
            values = (
                bx + half_step * (bu + new_u) - FAR_SHIFT,
                by + half_step * (bv + new_v) - FAR_SHIFT,
                new_u,
                new_v,
                new_rho,
            )
            least = jnp.min(jnp.where(occupied, new_rho, EMPTY_DENSITY), axis=0, keepdims=True)
            lowest = least if lowest is None else jnp.minimum(lowest, least)
        else:
            values = (
                padded[0, i + 1, own, :] + half_step * u,
                padded[1, i + 1, own, :] + half_step * v,
                u + half_step * force_x,
                v + half_step * force_y,
                padded[4, i + 1, own, :] + half_step * compress,
            )
        for k, value in enumerate(values):
            out[k, i] = jnp.where(occupied, value, 0.0)
    if final:
        low[...] = jnp.broadcast_to(lowest, low.shape)


def rates_step(padded, base=None):
    count, pcols, prows, slots = padded.shape
    cols, rows = pcols - 2, prows - 2
    final = base is not None
    out_shape = [jax.ShapeDtypeStruct((count, cols, rows, slots), jnp.float32)]
    if final:
        out_shape.append(jax.ShapeDtypeStruct((8, slots), jnp.float32))
    operands = (padded, base) if final else (padded,)
    vmem = pl.BlockSpec(memory_space=pltpu.VMEM)
    pairs = 9 * cols * rows * slots * slots
    return pl.pallas_call(
        functools.partial(rates_kernel, final),
        out_shape=out_shape,
        in_specs=[vmem] * len(operands),
        out_specs=[vmem] * len(out_shape),
        scratch_shapes=[
            pltpu.VMEM((pcols, prows, slots), jnp.float32),
            pltpu.VMEM((pcols, prows, slots), jnp.float32),
            pltpu.VMEM((prows, QROWS, slots), jnp.float32),
            pltpu.VMEM((pcols, QROWS, prows * slots), jnp.bfloat16),
            pltpu.VMEM((cols * rows, QROWS, slots), jnp.float32),
        ],
        compiler_params=pltpu.CompilerParams(vmem_limit_bytes=32 * 1024 * 1024),
        cost_estimate=pl.CostEstimate(
            flops=pairs * 40, bytes_accessed=4 * 1024 * 1024, transcendentals=pairs
        ),
    )(*operands)


def body(positions, velocity, density, counts):
    slot_index = jnp.arange(positions.shape[-1], dtype=jnp.int32)
    occupied = slot_index[None, None, :] < counts[:, :, None]
    fields = jnp.concatenate([positions + FAR_SHIFT, velocity, density[None]], axis=0)
    fields = jnp.where(occupied[None], fields, 0.0)
    (predicted,) = rates_step(extend_rims(fields))
    new_fields, low = rates_step(extend_rims(predicted), fields)
    lowest = lax.pmin(jnp.min(low), ("chan", "cross"))
    return (new_fields, lowest)


def solution(mesh):
    return jax.shard_map(
        body,
        mesh=mesh,
        in_specs=(
            P(None, "chan", "cross", None),
            P(None, "chan", "cross", None),
            P("chan", "cross", None),
            P("chan", "cross"),
        ),
        out_specs=(P(None, "chan", "cross", None), P()),
        check_vma=False,
    )
```

```python
import functools
import math

import jax
import jax.numpy as jnp
from jax import lax
from jax.experimental import pallas as pl
from jax.experimental.pallas import tpu as pltpu
from jax.sharding import PartitionSpec as P

FAR_SHIFT = 8.0
SOUND_SQ = 100.0
KERNEL_GRAD = 140.0 / math.pi
PARTICLE_MASS = 1.0 / 128.0
GRAVITY = 1.0
TIME_STEP = 0.025
FORCE_SCALE = KERNEL_GRAD * PARTICLE_MASS
EMPTY_DENSITY = 1000000000.0

FEATURES = 9
QROWS = 32
MESH = pl.DeviceIdType.MESH
BINS_AT_ONCE = 2
CHUNK = 32


def halo_kernel(fields, padded, top, bottom, land_chan, land_cross, send_sems, recv_sems):
    _, cols, rows, _ = fields.shape
    chan, cross = lax.axis_index("chan"), lax.axis_index("cross")
    chans, crosses = lax.axis_size("chan"), lax.axis_size("cross")
    around = [lax.rem(chan + (chans - 1), chans), chan, lax.rem(chan + 1, chans)]
    above, below = lax.rem(cross + 1, crosses), lax.rem(cross + (crosses - 1), crosses)
    has_above, has_below = cross < crosses - 1, cross > 0

    barrier = pltpu.get_barrier_semaphore()
    for place in (around[0], around[2]):
        pl.semaphore_signal(barrier, inc=1, device_id=(place, cross), device_id_type=MESH)
    for there, row in ((has_above, above), (has_below, below)):
        @pl.when(there)
        def _():
            for place in around:
                pl.semaphore_signal(barrier, inc=1, device_id=(place, row), device_id_type=MESH)

    top[...] = jnp.zeros_like(top)
    bottom[...] = jnp.zeros_like(bottom)
    top[:, 0:cols, :] = fields[:, :, rows - 1, :]
    bottom[:, 0:cols, :] = fields[:, :, 0, :]
    pl.semaphore_wait(
        barrier, 2 + 3 * has_above.astype(jnp.int32) + 3 * has_below.astype(jnp.int32)
    )

    def remote(src, dst, slot, place, row):
        return pltpu.make_async_remote_copy(
            src_ref=src,
            dst_ref=dst,
            send_sem=send_sems.at[slot],
            recv_sem=recv_sems.at[slot],
            device_id=(place, row),
            device_id_type=MESH,
        )

    upward = [remote(top, land_cross.at[k], k, around[2 - k], above) for k in range(3)]
    downward = [remote(bottom, land_cross.at[3 + k], 3 + k, around[2 - k], below) for k in range(3)]
    sideways = [
        remote(fields.at[:, cols - 1], land_chan.at[0], 6, around[2], cross),
        remote(fields.at[:, 0], land_chan.at[1], 7, around[0], cross),
    ]

    @pl.when(has_above)
    def _():
        for copy in upward:
            copy.start()

    @pl.when(has_below)
    def _():
        for copy in downward:
            copy.start()

    for copy in sideways:
        copy.start()

    padded[:, 1 : cols + 1, 1 : rows + 1, :] = fields[...]
    for copy in sideways:
        copy.wait()
    padded[:, 0, 1 : rows + 1, :] = land_chan[0]
    padded[:, cols + 1, 1 : rows + 1, :] = land_chan[1]

    for here, there, arriving, leaving, first, rim in (
        (has_below, has_above, upward, upward, 0, 0),
        (has_above, has_below, downward, downward, 3, rows + 1),
    ):
        @pl.when(here)
        def _():
            for copy in arriving:
                copy.wait_recv()
            padded[:, 0, rim, :] = land_cross[first, :, cols - 1, :]
            padded[:, 1 : cols + 1, rim, :] = land_cross[first + 1, :, 0:cols, :]
            padded[:, cols + 1, rim, :] = land_cross[first + 2, :, 0, :]

        @pl.when(jnp.logical_not(here))
        def _():
            padded[:, :, rim, :] = jnp.zeros_like(padded[:, :, rim, :])

        @pl.when(there)
        def _():
            for copy in leaving:
                copy.wait_send()


def extend_rims(fields, collective_id):
    count, cols, rows, slots = fields.shape
    sublanes = -(-cols // 8) * 8
    vmem = pl.BlockSpec(memory_space=pltpu.VMEM)
    return pl.pallas_call(
        halo_kernel,
        out_shape=jax.ShapeDtypeStruct((count, cols + 2, rows + 2, slots), jnp.float32),
        in_specs=[vmem],
        out_specs=vmem,
        scratch_shapes=[
            pltpu.VMEM((count, sublanes, slots), jnp.float32),
            pltpu.VMEM((count, sublanes, slots), jnp.float32),
            pltpu.VMEM((2, count, rows, slots), jnp.float32),
            pltpu.VMEM((6, count, sublanes, slots), jnp.float32),
            pltpu.SemaphoreType.DMA((8,)),
            pltpu.SemaphoreType.DMA((8,)),
        ],
        compiler_params=pltpu.CompilerParams(collective_id=collective_id, has_side_effects=True),
    )(fields)


def lowest_kernel(low, out, mine, land_chan, land_cross, send_sems, recv_sems):
    chan, cross = lax.axis_index("chan"), lax.axis_index("cross")
    chans, crosses = lax.axis_size("chan"), lax.axis_size("cross")
    along = [(lax.rem(chan + k, chans), cross) for k in range(1, chans)]
    across = [(chan, lax.rem(cross + k, crosses)) for k in range(1, crosses)]
    barrier = pltpu.get_barrier_semaphore()
    for place in along + across:
        pl.semaphore_signal(barrier, inc=1, device_id=place, device_id_type=MESH)
    pl.semaphore_wait(barrier, len(along) + len(across))

    def gather(src, land, first, places):
        copies = [
            pltpu.make_async_remote_copy(
                src_ref=src,
                dst_ref=land.at[k],
                send_sem=send_sems.at[first + k],
                recv_sem=recv_sems.at[first + k],
                device_id=place,
                device_id_type=MESH,
            )
            for k, place in enumerate(places)
        ]
        for copy in copies:
            copy.start()
        for copy in copies:
            copy.wait()
        least = src[...]
        for k in range(len(places)):
            least = jnp.minimum(least, land[k])
        return least

    mine[...] = gather(low, land_chan, 0, along)
    least = gather(mine, land_cross, len(along), across)
    out[...] = jnp.broadcast_to(jnp.min(least, keepdims=True), out.shape)


def lowest_everywhere(low, collective_id):
    chans, crosses = lax.axis_size("chan"), lax.axis_size("cross")
    vmem = pl.BlockSpec(memory_space=pltpu.VMEM)
    peers = chans + crosses - 2
    return pl.pallas_call(
        lowest_kernel,
        out_shape=jax.ShapeDtypeStruct(low.shape, jnp.float32),
        in_specs=[vmem],
        out_specs=vmem,
        scratch_shapes=[
            pltpu.VMEM(low.shape, jnp.float32),
            pltpu.VMEM((chans - 1,) + low.shape, jnp.float32),
            pltpu.VMEM((crosses - 1,) + low.shape, jnp.float32),
            pltpu.SemaphoreType.DMA((peers,)),
            pltpu.SemaphoreType.DMA((peers,)),
        ],
        compiler_params=pltpu.CompilerParams(collective_id=collective_id, has_side_effects=True),
    )(low)


def split3(value):
    high = value.astype(jnp.bfloat16).astype(jnp.float32)
    rest = value - high
    middle = rest.astype(jnp.bfloat16).astype(jnp.float32)
    return high, middle, rest - middle


def rates_kernel(final, *refs):
    if final:
        padded, base, out, low, px, py, staged, feats, sums = refs
    else:
        padded, out, px, py, staged, feats, sums = refs
    _, pcols, prows, slots = padded.shape
    cols, rows = pcols - 2, prows - 2
    mid_col, mid_row = (pcols - 1) / 2.0, (prows - 1) / 2.0

    row_shift = lax.broadcasted_iota(jnp.int32, (prows, slots), 0).astype(jnp.float32) - mid_row
    staged[...] = jnp.zeros_like(staged)
    for c in range(pcols):
        x = (padded[0, c] - (FAR_SHIFT + 0.5)) + (c - mid_col)
        y = (padded[1, c] - (FAR_SHIFT + 0.5)) + row_shift
        u, v = padded[2, c], padded[3, c]
        p = SOUND_SQ * (padded[4, c] - 1.0)
        px[c] = x
        py[c] = y
        staged[:, 0, :] = jnp.ones_like(x)
        for f, value in enumerate((x, y, p, p * x, p * y, u, v, u * x + v * y)):
            for k, part in enumerate(split3(value)):
                staged[:, 1 + 3 * f + k, :] = part
        for j in range(prows):
            feats[c, :, j * slots : (j + 1) * slots] = staged[j].astype(jnp.bfloat16)

    at_once = math.gcd(BINS_AT_ONCE, cols * rows)

    def some_bins(step, carry):
        places = []
        for k in range(at_once):
            n = step * at_once + k
            i, j = n // rows, n % rows
            xa = jnp.broadcast_to(px[i + 1, pl.ds(j + 1, 1), :], (slots, slots)).T
            ya = jnp.broadcast_to(py[i + 1, pl.ds(j + 1, 1), :], (slots, slots)).T
            places.append((n, i, j, xa, ya))
        totals = [None] * at_once
        for di in range(3):
            for k, (n, i, j, xa, ya) in enumerate(places):
                xb = [px[i + di, pl.ds(j + dj, 1), :] for dj in range(3)]
                yb = [py[i + di, pl.ds(j + dj, 1), :] for dj in range(3)]
                weights = []
                for a in range(0, slots, CHUNK):
                    highs, lows = [], []
                    for dj in range(3):
                        dx = xa[a : a + CHUNK] - xb[dj]
                        dy = ya[a : a + CHUNK] - yb[dj]
                        d2 = jnp.maximum(dx * dx + dy * dy, 1e-30)
                        s = jnp.maximum(1.0 - d2 * lax.rsqrt(d2), 0.0)
                        w = s * s * s
                        high = w.astype(jnp.bfloat16)
                        highs.append(high)
                        lows.append((w - high.astype(jnp.float32)).astype(jnp.bfloat16))
                    weights.append(jnp.concatenate(highs + lows, axis=1))
                q = feats[i + di, :, pl.ds(pl.multiple_of(j * slots, slots), 3 * slots)]
                part = lax.dot_general(
                    jnp.concatenate(weights, axis=0),
                    jnp.concatenate([q, q], axis=1),
                    (((1,), (1,)), ((), ())),
                    preferred_element_type=jnp.float32,
                )
                totals[k] = part if di == 0 else totals[k] + part
        for k, (n, i, j, xa, ya) in enumerate(places):
            sums[n] = totals[k].T
        return carry

    lax.fori_loop(0, cols * rows // at_once, some_bins, 0)

    lowest = None
    for i in range(cols):
        def take(f):
            block = pl.ds(i * rows, rows)
            if f == 0:
                return sums[block, 0, :]
            first = 1 + 3 * (f - 1)
            return sums[block, first, :] + (sums[block, first + 1, :] + sums[block, first + 2, :])

        s1, sx, sy, sp, spx, spy, su, sv, sc = [take(f) for f in range(FEATURES)]
        own = pl.ds(1, rows)
        x, y = px[i + 1, own, :], py[i + 1, own, :]
        u, v = padded[2, i + 1, own, :], padded[3, i + 1, own, :]
        p = SOUND_SQ * (padded[4, i + 1, own, :] - 1.0)
        away_x, away_y = x * s1 - sx, y * s1 - sy
        force_x = FORCE_SCALE * (p * away_x + (x * sp - spx))
        force_y = FORCE_SCALE * (p * away_y + (y * sp - spy)) - GRAVITY
        compress = -FORCE_SCALE * ((u * away_x + v * away_y) - (x * su + y * sv) + sc)
        occupied = padded[0, i + 1, own, :] > 0.5 * FAR_SHIFT
        half_step = 0.5 * TIME_STEP
        if final:
            bx, by, bu, bv, br = [base[k, i] for k in range(5)]
            new_u = bu + TIME_STEP * force_x
            new_v = bv + TIME_STEP * force_y
            new_rho = br + TIME_STEP * compress
            values = (
                bx + half_step * (bu + new_u) - FAR_SHIFT,
                by + half_step * (bv + new_v) - FAR_SHIFT,
                new_u,
                new_v,
                new_rho,
            )
            least = jnp.min(jnp.where(occupied, new_rho, EMPTY_DENSITY), axis=0, keepdims=True)
            lowest = least if lowest is None else jnp.minimum(lowest, least)
        else:
            values = (
                padded[0, i + 1, own, :] + half_step * u,
                padded[1, i + 1, own, :] + half_step * v,
                u + half_step * force_x,
                v + half_step * force_y,
                padded[4, i + 1, own, :] + half_step * compress,
            )
        for k, value in enumerate(values):
            out[k, i] = jnp.where(occupied, value, 0.0)
    if final:
        low[...] = jnp.broadcast_to(lowest, low.shape)


def rates_step(padded, base=None):
    count, pcols, prows, slots = padded.shape
    cols, rows = pcols - 2, prows - 2
    final = base is not None
    out_shape = [jax.ShapeDtypeStruct((count, cols, rows, slots), jnp.float32)]
    if final:
        out_shape.append(jax.ShapeDtypeStruct((8, slots), jnp.float32))
    operands = (padded, base) if final else (padded,)
    vmem = pl.BlockSpec(memory_space=pltpu.VMEM)
    pairs = 9 * cols * rows * slots * slots
    return pl.pallas_call(
        functools.partial(rates_kernel, final),
        out_shape=out_shape,
        in_specs=[vmem] * len(operands),
        out_specs=[vmem] * len(out_shape),
        scratch_shapes=[
            pltpu.VMEM((pcols, prows, slots), jnp.float32),
            pltpu.VMEM((pcols, prows, slots), jnp.float32),
            pltpu.VMEM((prows, QROWS, slots), jnp.float32),
            pltpu.VMEM((pcols, QROWS, prows * slots), jnp.bfloat16),
            pltpu.VMEM((cols * rows, QROWS, slots), jnp.float32),
        ],
        compiler_params=pltpu.CompilerParams(vmem_limit_bytes=32 * 1024 * 1024),
        cost_estimate=pl.CostEstimate(
            flops=pairs * 40, bytes_accessed=4 * 1024 * 1024, transcendentals=pairs
        ),
    )(*operands)


def body(positions, velocity, density, counts):
    slot_index = jnp.arange(positions.shape[-1], dtype=jnp.int32)
    occupied = slot_index[None, None, :] < counts[:, :, None]
    fields = jnp.concatenate([positions + FAR_SHIFT, velocity, density[None]], axis=0)
    fields = jnp.where(occupied[None], fields, 0.0)
    (predicted,) = rates_step(extend_rims(fields, 0))
    new_fields, low = rates_step(extend_rims(predicted, 1), fields)
    return (new_fields, lowest_everywhere(low, 2)[0, 0])


def solution(mesh):
    return jax.shard_map(
        body,
        mesh=mesh,
        in_specs=(
            P(None, "chan", "cross", None),
            P(None, "chan", "cross", None),
            P("chan", "cross", None),
            P("chan", "cross"),
        ),
        out_specs=(P(None, "chan", "cross", None), P()),
        check_vma=False,
    )
```

```python
import math

import jax
import jax.numpy as jnp
from jax import lax
from jax.experimental import pallas as pl
from jax.experimental.pallas import tpu as pltpu
from jax.sharding import PartitionSpec as P

FAR_SHIFT = 8.0
SOUND_SQ = 100.0
KERNEL_GRAD = 140.0 / math.pi
PARTICLE_MASS = 1.0 / 128.0
GRAVITY = 1.0
TIME_STEP = 0.025
FORCE_SCALE = KERNEL_GRAD * PARTICLE_MASS
EMPTY_DENSITY = 1000000000.0

FEATURES = 9
QROWS = 32
MESH = pl.DeviceIdType.MESH
BINS_AT_ONCE = 2
CHUNK = 32


def split3(value):
    high = value.astype(jnp.bfloat16).astype(jnp.float32)
    rest = value - high
    middle = rest.astype(jnp.bfloat16).astype(jnp.float32)
    return high, middle, rest - middle


def step_kernel(
    fields, out, low, padded, predicted, tops, bottoms, lands_chan, lands_cross,
    px, py, staged, feats, sums, mine, low_chan, low_cross,
    send_sems, recv_sems, low_send, low_recv,
):
    _, cols, rows, slots = fields.shape
    pcols, prows = cols + 2, rows + 2
    mid_col, mid_row = (pcols - 1) / 2.0, (prows - 1) / 2.0
    chan, cross = lax.axis_index("chan"), lax.axis_index("cross")
    chans, crosses = lax.axis_size("chan"), lax.axis_size("cross")
    around = [lax.rem(chan + (chans - 1), chans), chan, lax.rem(chan + 1, chans)]
    above, below = lax.rem(cross + 1, crosses), lax.rem(cross + (crosses - 1), crosses)
    has_above, has_below = cross < crosses - 1, cross > 0
    along = [(lax.rem(chan + k, chans), cross) for k in range(1, chans)]
    across = [(chan, lax.rem(cross + k, crosses)) for k in range(1, crosses)]

    barrier = pltpu.get_barrier_semaphore()
    for place in along + across:
        pl.semaphore_signal(barrier, inc=1, device_id=place, device_id_type=MESH)
    for there, row in ((has_above, above), (has_below, below)):
        @pl.when(there)
        def _():
            for place in (around[0], around[2]):
                pl.semaphore_signal(barrier, inc=1, device_id=(place, row), device_id_type=MESH)

    def remote(src, dst, send, recv, place):
        return pltpu.make_async_remote_copy(
            src_ref=src, dst_ref=dst, send_sem=send, recv_sem=recv,
            device_id=place, device_id_type=MESH,
        )

    def halo(source, stage):
        top, bottom = tops.at[stage], bottoms.at[stage]
        land_chan, land_cross = lands_chan.at[stage], lands_cross.at[stage]

        def one(src, dst, slot, place):
            return remote(src, dst, send_sems.at[stage, slot], recv_sems.at[stage, slot], place)

        upward = [one(top, land_cross.at[k], k, (around[2 - k], above)) for k in range(3)]
        downward = [
            one(bottom, land_cross.at[3 + k], 3 + k, (around[2 - k], below)) for k in range(3)
        ]
        sideways = [
            one(source.at[:, cols - 1], land_chan.at[0], 6, (around[2], cross)),
            one(source.at[:, 0], land_chan.at[1], 7, (around[0], cross)),
        ]
        return upward, downward, sideways

    def fill_rims(source, stage):
        top, bottom = tops.at[stage], bottoms.at[stage]
        top[...] = jnp.zeros_like(top)
        bottom[...] = jnp.zeros_like(bottom)
        top[:, 0:cols, :] = source[:, :, rows - 1, :]
        bottom[:, 0:cols, :] = source[:, :, 0, :]

    def send(copies):
        upward, downward, sideways = copies

        @pl.when(has_above)
        def _():
            for copy in upward:
                copy.start()

        @pl.when(has_below)
        def _():
            for copy in downward:
                copy.start()

        for copy in sideways:
            copy.start()

    def receive(copies, stage):
        upward, downward, sideways = copies
        land_chan, land_cross = lands_chan.at[stage], lands_cross.at[stage]
        for copy in sideways:
            copy.wait()
        padded[:, 0, 1 : rows + 1, :] = land_chan[0]
        padded[:, cols + 1, 1 : rows + 1, :] = land_chan[1]
        for here, there, moving, first, rim in (
            (has_below, has_above, upward, 0, 0),
            (has_above, has_below, downward, 3, rows + 1),
        ):
            @pl.when(here)
            def _():
                for copy in moving:
                    copy.wait_recv()
                padded[:, 0, rim, :] = land_cross[first, :, cols - 1, :]
                padded[:, 1 : cols + 1, rim, :] = land_cross[first + 1, :, 0:cols, :]
                padded[:, cols + 1, rim, :] = land_cross[first + 2, :, 0, :]

            @pl.when(there)
            def _():
                for copy in moving:
                    copy.wait_send()

    row_shift = lax.broadcasted_iota(jnp.int32, (prows, slots), 0).astype(jnp.float32) - mid_row

    def build(first, last):
        for c in range(first, last):
            x = (padded[0, c] - (FAR_SHIFT + 0.5)) + (c - mid_col)
            y = (padded[1, c] - (FAR_SHIFT + 0.5)) + row_shift
            u, v = padded[2, c], padded[3, c]
            p = SOUND_SQ * (padded[4, c] - 1.0)
            px[c] = x
            py[c] = y
            staged[:, 0, :] = jnp.ones_like(x)
            for f, value in enumerate((x, y, p, p * x, p * y, u, v, u * x + v * y)):
                for k, part in enumerate(split3(value)):
                    staged[:, 1 + 3 * f + k, :] = part
            for j in range(prows):
                feats[c, :, j * slots : (j + 1) * slots] = staged[j].astype(jnp.bfloat16)

    def sum_bins(count, bin_of):
        at_once = math.gcd(BINS_AT_ONCE, count)

        def some_bins(step, carry):
            places = []
            for k in range(at_once):
                i, j = bin_of(step * at_once + k)
                xa = jnp.broadcast_to(px[i + 1, pl.ds(j + 1, 1), :], (slots, slots)).T
                ya = jnp.broadcast_to(py[i + 1, pl.ds(j + 1, 1), :], (slots, slots)).T
                places.append((i, j, jnp.concatenate([xa] * 3, 1), jnp.concatenate([ya] * 3, 1)))
            totals = [None] * at_once
            for di in range(3):
                for k, (i, j, xa, ya) in enumerate(places):
                    xb = jnp.concatenate([px[i + di, pl.ds(j + dj, 1), :] for dj in range(3)], 1)
                    yb = jnp.concatenate([py[i + di, pl.ds(j + dj, 1), :] for dj in range(3)], 1)
                    weights = []
                    for a in range(0, slots, CHUNK):
                        dx = xa[a : a + CHUNK] - xb
                        dy = ya[a : a + CHUNK] - yb
                        d2 = jnp.maximum(dx * dx + dy * dy, 1e-30)
                        s = jnp.maximum(1.0 - d2 * lax.rsqrt(d2), 0.0)
                        w = s * s * s
                        high = w.astype(jnp.bfloat16)
                        low_part = (w - high.astype(jnp.float32)).astype(jnp.bfloat16)
                        weights.append(jnp.concatenate([high, low_part], axis=1))
                    q = feats[i + di, :, pl.ds(pl.multiple_of(j * slots, slots), 3 * slots)]
                    part = lax.dot_general(
                        jnp.concatenate(weights, axis=0),
                        jnp.concatenate([q, q], axis=1),
                        (((1,), (1,)), ((), ())),
                        preferred_element_type=jnp.float32,
                    )
                    totals[k] = part if di == 0 else totals[k] + part
            for k, (i, j, xa, ya) in enumerate(places):
                sums[i * rows + j] = totals[k].T
            return carry

        lax.fori_loop(0, count // at_once, some_bins, 0)

    def inner(n):
        return 1 + n // (rows - 2), 1 + n % (rows - 2)

    def sides(n):
        return (n // rows) * (cols - 1), n % rows

    def ends(n):
        return 1 + n // 2, (n % 2) * (rows - 1)

    def rates(i):
        def take(f):
            block = pl.ds(i * rows, rows)
            if f == 0:
                return sums[block, 0, :]
            first = 1 + 3 * (f - 1)
            return sums[block, first, :] + (sums[block, first + 1, :] + sums[block, first + 2, :])

        s1, sx, sy, sp, spx, spy, su, sv, sc = [take(f) for f in range(FEATURES)]
        own = pl.ds(1, rows)
        x, y = px[i + 1, own, :], py[i + 1, own, :]
        u, v = padded[2, i + 1, own, :], padded[3, i + 1, own, :]
        p = SOUND_SQ * (padded[4, i + 1, own, :] - 1.0)
        away_x, away_y = x * s1 - sx, y * s1 - sy
        force_x = FORCE_SCALE * (p * away_x + (x * sp - spx))
        force_y = FORCE_SCALE * (p * away_y + (y * sp - spy)) - GRAVITY
        compress = -FORCE_SCALE * ((u * away_x + v * away_y) - (x * su + y * sv) + sc)
        return force_x, force_y, compress

    def one_pass(source, stage):
        copies = halo(source, stage)
        fill_rims(source, stage)
        if stage == 0:
            pl.semaphore_wait(
                barrier,
                len(along) + len(across)
                + 2 * has_above.astype(jnp.int32) + 2 * has_below.astype(jnp.int32),
            )
        send(copies)
        padded[:, 1 : cols + 1, 1 : rows + 1, :] = source[...]
        build(1, cols + 1)
        sum_bins((cols - 2) * (rows - 2), inner)
        receive(copies, stage)
        build(0, pcols)
        sum_bins(2 * rows, sides)
        sum_bins(2 * (cols - 2), ends)

    half_step = 0.5 * TIME_STEP
    staged[...] = jnp.zeros_like(staged)
    padded[...] = jnp.zeros_like(padded)

    one_pass(fields, 0)
    for i in range(cols):
        force_x, force_y, compress = rates(i)
        x, y, u, v, rho = [fields[k, i] for k in range(5)]
        values = (
            x + half_step * u,
            y + half_step * v,
            u + half_step * force_x,
            v + half_step * force_y,
            rho + half_step * compress,
        )
        for k, value in enumerate(values):
            predicted[k, i] = jnp.where(x > 0.5 * FAR_SHIFT, value, 0.0)

    one_pass(predicted, 1)
    lowest = None
    for i in range(cols):
        force_x, force_y, compress = rates(i)
        x, y, u, v, rho = [fields[k, i] for k in range(5)]
        occupied = x > 0.5 * FAR_SHIFT
        new_u, new_v = u + TIME_STEP * force_x, v + TIME_STEP * force_y
        new_rho = rho + TIME_STEP * compress
        values = (
            x + half_step * (u + new_u) - FAR_SHIFT,
            y + half_step * (v + new_v) - FAR_SHIFT,
            new_u,
            new_v,
            new_rho,
        )
        for k, value in enumerate(values):
            out[k, i] = jnp.where(occupied, value, 0.0)
        least = jnp.min(jnp.where(occupied, new_rho, EMPTY_DENSITY), axis=0, keepdims=True)
        lowest = least if lowest is None else jnp.minimum(lowest, least)

    def gather(src, land, first, places):
        copies = [
            remote(src, land.at[k], low_send.at[first + k], low_recv.at[first + k], place)
            for k, place in enumerate(places)
        ]
        for copy in copies:
            copy.start()
        for copy in copies:
            copy.wait()
        least = src[...]
        for k in range(len(places)):
            least = jnp.minimum(least, land[k])
        return least

    mine[0] = jnp.broadcast_to(lowest, mine.shape[1:])
    mine[1] = gather(mine.at[0], low_chan, 0, along)
    least = gather(mine.at[1], low_cross, len(along), across)
    low[...] = jnp.broadcast_to(jnp.min(least, keepdims=True), low.shape)


def whole_step(fields):
    count, cols, rows, slots = fields.shape
    pcols, prows = cols + 2, rows + 2
    sublanes = -(-cols // 8) * 8
    chans, crosses = lax.axis_size("chan"), lax.axis_size("cross")
    peers = chans + crosses - 2
    vmem = pl.BlockSpec(memory_space=pltpu.VMEM)
    pairs = 2 * 9 * cols * rows * slots * slots
    held = [
        (count, pcols, prows, slots),
        (count, cols, rows, slots),
        (2, count, sublanes, slots),
        (2, count, sublanes, slots),
        (2, 2, count, rows, slots),
        (2, 6, count, sublanes, slots),
        (pcols, prows, slots),
        (pcols, prows, slots),
        (prows, QROWS, slots),
    ]
    return pl.pallas_call(
        step_kernel,
        out_shape=[
            jax.ShapeDtypeStruct(fields.shape, jnp.float32),
            jax.ShapeDtypeStruct((8, slots), jnp.float32),
        ],
        in_specs=[vmem],
        out_specs=[vmem, vmem],
        scratch_shapes=[pltpu.VMEM(shape, jnp.float32) for shape in held]
        + [
            pltpu.VMEM((pcols, QROWS, prows * slots), jnp.bfloat16),
            pltpu.VMEM((cols * rows, QROWS, slots), jnp.float32),
            pltpu.VMEM((2, 8, slots), jnp.float32),
            pltpu.VMEM((chans - 1, 8, slots), jnp.float32),
            pltpu.VMEM((crosses - 1, 8, slots), jnp.float32),
            pltpu.SemaphoreType.DMA((2, 8)),
            pltpu.SemaphoreType.DMA((2, 8)),
            pltpu.SemaphoreType.DMA((peers,)),
            pltpu.SemaphoreType.DMA((peers,)),
        ],
        compiler_params=pltpu.CompilerParams(
            collective_id=0, has_side_effects=True, vmem_limit_bytes=32 * 1024 * 1024
        ),
        cost_estimate=pl.CostEstimate(
            flops=pairs * 40, bytes_accessed=4 * 1024 * 1024, transcendentals=pairs
        ),
    )(fields)


def body(positions, velocity, density, counts):
    slot_index = jnp.arange(positions.shape[-1], dtype=jnp.int32)
    occupied = slot_index[None, None, :] < counts[:, :, None]
    fields = jnp.concatenate([positions + FAR_SHIFT, velocity, density[None]], axis=0)
    fields = jnp.where(occupied[None], fields, 0.0)
    new_fields, low = whole_step(fields)
    return (new_fields, low[0, 0])


def solution(mesh):
    return jax.shard_map(
        body,
        mesh=mesh,
        in_specs=(
            P(None, "chan", "cross", None),
            P(None, "chan", "cross", None),
            P("chan", "cross", None),
            P("chan", "cross"),
        ),
        out_specs=(P(None, "chan", "cross", None), P()),
        check_vma=False,
    )
```
